32 devices in a mesh: dp: 8 (over z, core), filter: 4 (over y, x).
Axes of the slice: x: 2, y: 2, z: 4, core: 2. Of those that a mesh axis runs over, the one named last changes fastest.
Arguments:
- patches: bfloat16 [256, 24, 2048], P('filter', 'dp'), may hold values from -6 to 6
- cotangent: bfloat16 [256, 24, 2048], P('filter', 'dp'), may hold values from -6 to 6
- first_weight: bfloat16 [27, 256, 256], P(None, 'filter'), may hold values from -0.078125 to 0.078125
- second_weight: bfloat16 [27, 256, 256], P(None, 'filter'), may hold values from -0.078125 to 0.078125
- counts: int32 [8], P('dp'), may hold values from 0 to 3, as said below
Outputs:
- output_maps: float32 [256, 24, 2048], P('filter', 'dp')
- input_grad: float32 [256, 24, 2048], P('filter', 'dp')
- first_grad: float32 [27, 256, 256], P(None, 'filter')
- second_grad: float32 [27, 256, 256], P(None, 'filter')
The draws below stay inside these ranges and needn't reach their ends.
Inputs may be any that keep to these rules, and one draw needn't show every extreme that they name: The counts of all groups sum to 8; one group holds exactly 3 live patches. Live patches of a group occupy its first slots.
All inputs are finite; a program needn't handle non-finite values.
Results may differ from the reference program's by a relative error of at most 0.0029.
Values may be sent and summed in bfloat16 or wider, within the bound.
A program may use at most 192 MiB of HBM per device.

```python
import jax
import jax.numpy as jnp
from jax import lax

C = 256
PX = 8
PY = 16
PZ = 16
CAP = 3
CELLS = 2048
SLOTS = 24
N_DP = 8


def draw_counts(key, part):
    order = jax.random.permutation(key, N_DP)
    counts = jnp.ones((N_DP,), jnp.int32)
    counts = counts.at[order[0]].set(CAP).at[order[1]].set(0).at[order[2]].set(0)
    pairs = (N_DP - 3) // 2
    if pairs > 0:
        flips = jax.random.randint(jax.random.fold_in(key, 1), (pairs,), 0, 2).astype(jnp.int32)
        counts = counts.at[order[3:3 + 2 * pairs:2]].add(flips)
        counts = counts.at[order[4:4 + 2 * pairs:2]].add(-flips)
    return counts


def block_scale(rng, extent, split, low, top_value):
    def one(axis_at, blocks):
        draws = jax.random.uniform(jax.random.fold_in(jax.random.fold_in(rng, 6), axis_at), (blocks,), jnp.float32, low / len(split), top_value / len(split))
        return jnp.repeat(jnp.exp(draws), extent[axis_at] // blocks).reshape((-1,) + (1,) * (len(extent) - axis_at - 1))

    loudness = one(*split[0])
    for cut in split[1:]:
        loudness = loudness * one(*cut)
    return loudness


def gaussian(rng, extent, scale, most, pieces=(), kind=jnp.bfloat16):
    level = block_scale(rng, extent, pieces, -0.22, 0.18) if pieces else 1.0
    values = jax.random.normal(rng, extent, jnp.float32) * scale * level
    return jnp.minimum(jnp.maximum(values, -most), most).astype(kind)


def setup_inputs(seed: int = 0) -> dict:
    arg_keys = jax.random.split(jax.random.key(seed), 6)
    return {
        "patches": gaussian(arg_keys[0], (C, SLOTS, CELLS), 1.0, 6.0, ((0, 4), (1, 8))),
        "cotangent": gaussian(arg_keys[1], (C, SLOTS, CELLS), 1.0, 6.0, ((0, 4), (1, 8))),
        "first_weight": gaussian(arg_keys[2], (27, C, C), (27 * C) ** -0.5, 0.078125, ((1, 4),)),
        "second_weight": gaussian(arg_keys[3], (27, C, C), (27 * C) ** -0.5, 0.078125, ((1, 4),)),
        "counts": draw_counts(jax.random.fold_in(arg_keys[5], 71), 0),
    }


stencil_taps = [(ox, oy, oz) for ox in (-1, 0, 1) for oy in (-1, 0, 1) for oz in (-1, 0, 1)]

def shift_cells(value, ox, oy, oz):
    span = PY * PZ + PZ + 1
    step = ox * PY * PZ + oy * PZ + oz
    padded = jnp.pad(value, [(0, 0)] * (value.ndim - 1) + [(span, span)])
    moved = lax.slice_in_dim(padded, span + step, span + step + CELLS, axis=value.ndim - 1)
    cell = jnp.arange(CELLS, dtype=jnp.int32)
    pos_x = cell // (PY * PZ) + ox
    pos_y = cell // PZ % PY + oy
    pos_z = cell % PZ + oz
    inside = (pos_x >= 0) & (pos_x < PX) & (pos_y >= 0) & (pos_y < PY) & (pos_z >= 0) & (pos_z < PZ)
    return jnp.where(inside, moved, jnp.zeros_like(moved))

def shifted_stack(value):
    return jnp.stack([shift_cells(value, -ox, -oy, -oz) for ox, oy, oz in stencil_taps])

def forward_conv(inputs, weight):
    proj = jnp.einsum('toi,isc->tosc', weight.astype(jnp.float32), inputs.astype(jnp.float32))
    total = jnp.zeros(proj.shape[1:], jnp.float32)
    for t, (ox, oy, oz) in enumerate(stencil_taps):
        total = total + shift_cells(proj[t], ox, oy, oz)
    return total

def backward_conv(grads, weight):
    stack = shifted_stack(grads).astype(jnp.float32)
    return jnp.einsum('toi,tosc->isc', weight.astype(jnp.float32), stack)

def weight_conv(grads, inputs):
    stack = shifted_stack(grads).astype(jnp.float32)
    return jnp.einsum('tosc,isc->toi', stack, inputs.astype(jnp.float32))

def reference(patches, cotangent, first_weight, second_weight, counts):
    live = (jnp.arange(CAP, dtype=jnp.int32)[None, :] < counts[:, None]).reshape(SLOTS)
    xs = jnp.moveaxis(patches, 1, 0)[:, :, None, :]
    gs = jnp.moveaxis(cotangent, 1, 0)[:, :, None, :]

    def one_slot(carry, item):
        acc_one, acc_two = carry
        inputs, grads, alive = item
        gate = jnp.where(alive, 1.0, 0.0).astype(jnp.float32)
        masked = (grads.astype(jnp.float32) * gate).astype(jnp.bfloat16)
        first = forward_conv(inputs, first_weight)
        hidden = jax.nn.silu(first).astype(jnp.bfloat16)
        out = forward_conv(hidden, second_weight) * gate
        hidden_grad = backward_conv(masked, second_weight)
        sg = jax.nn.sigmoid(first)
        delta = (hidden_grad * sg * (1.0 + first * (1.0 - sg))).astype(jnp.bfloat16)
        in_grad = backward_conv(delta, first_weight)
        acc_two = acc_two + weight_conv(masked, hidden)
        acc_one = acc_one + weight_conv(delta, inputs)
        return ((acc_one, acc_two), (out, in_grad))
    zeros = jnp.zeros((27, C, C), jnp.float32)
    (acc_one, acc_two), (outs, grads_in) = lax.scan(one_slot, (zeros, zeros), (xs, gs, live))
    scale = 1.0 / jnp.sqrt(jnp.float32(N_DP * CELLS))
    output_maps = jnp.moveaxis(outs[:, :, 0, :], 0, 1)
    input_grad = jnp.moveaxis(grads_in[:, :, 0, :], 0, 1)
    return (output_maps, input_grad, acc_one * scale, acc_two * scale)
```

```python
import functools
import math

import jax
import jax.numpy as jnp
from jax import lax
from jax.experimental import pallas as pl
from jax.experimental.pallas import tpu as pltpu
from jax.sharding import PartitionSpec as P

CAP = 3
CELLS = 2048
PLANE = 256
PLANES = 8
SIDE = 16
MESH = pl.DeviceIdType.MESH
F32 = jnp.float32
BF16 = jnp.bfloat16

PAIRS = [(oy, oz) for oy in (-1, 0, 1) for oz in (-1, 0, 1)]


def inside(oy, oz):
    cell = lax.broadcasted_iota(jnp.int32, (1, PLANE), 1)
    y = cell // SIDE + oy
    z = cell % SIDE + oz
    return (y >= 0) & (y < SIDE) & (z >= 0) & (z < SIDE)


def moved(value, oy, oz):
    step = oy * SIDE + oz
    if step == 0:
        return value
    rolled = pltpu.roll(value, (-step) % PLANE, 1)
    return jnp.where(inside(oy, oz), rolled, jnp.zeros_like(rolled))


def remote(src, dst, send, recv, target):
    return pltpu.make_async_remote_copy(
        src_ref=src, dst_ref=dst, send_sem=send, recv_sem=recv, device_id=target, device_id_type=MESH
    )


def build_stack(c, value, stack):
    zero = jnp.zeros((9 * c, PLANE), BF16)
    stack[0 : 9 * c, PLANES * PLANE : (PLANES + 1) * PLANE] = zero
    stack[18 * c : 27 * c, PLANE : 2 * PLANE] = zero

    def plane(p, _):
        part = value[:, pl.ds(pl.multiple_of(p * PLANE, PLANE), PLANE)].astype(F32)
        for j, (oy, oz) in enumerate(PAIRS):
            shifted = moved(part, -oy, -oz).astype(BF16)
            for ox in (-1, 0, 1):
                row = (9 * (ox + 1) + j) * c
                at = pl.multiple_of((p + ox + 1) * PLANE, PLANE)
                stack[row : row + c, pl.ds(at, PLANE)] = shifted
        return 0

    lax.fori_loop(0, PLANES, plane, 0)


def forward(c, value, weight, proj, finish):
    rows = 27 * c
    proj[0, 18 * c : rows, :] = jnp.zeros((9 * c, PLANE), F32)
    proj[0, 0 : 9 * c, :] = jnp.zeros((9 * c, PLANE), F32)
    proj[PLANES + 1, 18 * c : rows, :] = jnp.zeros((9 * c, PLANE), F32)

    def multiply(p, _):
        part = value[:, pl.ds(pl.multiple_of(p * PLANE, PLANE), PLANE)]
        proj[p + 1] = jnp.dot(weight[...], part, preferred_element_type=F32)
        return 0

    lax.fori_loop(0, PLANES, multiply, 0)

    def combine(q, _):
        total = jnp.zeros((c, PLANE), F32)
        for j, (oy, oz) in enumerate(PAIRS):
            terms = [
                proj[q + 1 + ox, (9 * (ox + 1) + j) * c : (9 * (ox + 1) + j + 1) * c, :] for ox in (-1, 0, 1)
            ]
            total = total + moved(terms[0] + terms[1] + terms[2], oy, oz)
        finish(q, total)
        return 0

    lax.fori_loop(0, PLANES, combine, 0)


def backward(weight_t, stack, out):
    def plane(q, _):
        part = stack[:, pl.ds(pl.multiple_of((q + 1) * PLANE, PLANE), PLANE)]
        value = jnp.dot(weight_t[...], part, preferred_element_type=F32)
        out[:, pl.ds(pl.multiple_of(q * PLANE, PLANE), PLANE)] = value.astype(out.dtype)
        return 0

    lax.fori_loop(0, PLANES, plane, 0)


def weight_grad(c, stack, value, out):
    for part in range(3):
        rows = pl.ds(part * 9 * c, 9 * c)
        out[rows, :] = lax.dot_general(
            stack[rows, PLANE : (PLANES + 1) * PLANE],
            value[...],
            (((1,), (1,)), ((), ())),
            preferred_element_type=F32,
        )
    rest = out.shape[0] - 27 * c
    if rest:
        out[27 * c :, :] = jnp.zeros((rest, out.shape[1]), F32)


def kernel(
    nf, nd, c, scale,
    x, u, w1, w2, w1t, w2t,
    out, igrad, g1, g2,
    xg, hg, stack, proj, hpart, hrecv, first, ipart, irecv, acc1, acc2, half1, half2, snd1, snd2, rcv1, rcv2,
    fs, fr, cs, cr, zs, zr,
):
    f = lax.axis_index("filter")
    d = lax.axis_index("dp")
    nz = nd // 2
    core = lax.rem(d, 2)
    z = d // 2
    mate = d + 1 - 2 * core

    def fpeer(k):
        return lax.rem(f + k, nf)

    def ffrom(k):
        return lax.rem(f + nf - k, nf)

    def zpeer(k):
        return lax.rem(z + k, nz)

    def zfrom(k):
        return lax.rem(z + nz - k, nz)

    barrier = pltpu.get_barrier_semaphore()
    for k in range(1, nf):
        pl.semaphore_signal(barrier, inc=1, device_id={"filter": fpeer(k)}, device_id_type=MESH)
    for k in range(1, nz):
        pl.semaphore_signal(barrier, inc=1, device_id={"dp": zpeer(k) * 2 + core}, device_id_type=MESH)
    pl.semaphore_signal(barrier, inc=1, device_id={"dp": mate}, device_id_type=MESH)
    pl.semaphore_wait(barrier, nf + nz - 1)

    def block(i):
        return pl.ds(pl.multiple_of(i * c, c), c)

    def gather(n, own, full):
        return [
            remote(own, full.at[block(f)], fs.at[n, k], fr.at[n, k], {"filter": fpeer(k)}) for k in range(1, nf)
        ]

    def gathered(n, own, full):
        for k in range(1, nf):
            remote(own, full.at[block(ffrom(k))], fs.at[n, k], fr.at[n, k], {"filter": fpeer(k)}).wait_recv()

    def scatter(n, part, recv):
        return [
            remote(part.at[block(fpeer(k))], recv.at[k], fs.at[n, k], fr.at[n, k], {"filter": fpeer(k)})
            for k in range(1, nf)
        ]

    copies = gather(0, x, xg)
    for copy in copies:
        copy.start()
    xg[block(f), :] = x[...]

    build_stack(c, u, stack)
    backward(w2t, stack, hpart)
    hcopies = scatter(1, hpart, hrecv)
    for copy in hcopies:
        copy.start()

    gathered(0, x, xg)

    def activate(q, total):
        at = pl.ds(pl.multiple_of(q * PLANE, PLANE), PLANE)
        first[:, at] = total
        hg[block(f), at] = (total / (1.0 + jnp.exp(-total))).astype(BF16)

    forward(c, xg, w1, proj, activate)
    own_hidden = hg.at[block(f)]
    gcopies = gather(2, own_hidden, hg)
    for copy in gcopies:
        copy.start()

    gathered(2, own_hidden, hg)
    weight_grad(c, stack, hg, acc2)

    half = acc1.shape[0] // 2
    chunk = half // nz

    def swap(n, acc, recv):
        return remote(
            acc.at[pl.ds(pl.multiple_of((1 - core) * half, half), half)],
            recv, cs.at[n], cr.at[n], {"dp": mate},
        )

    def spread(n, acc, recv, snd, rcv):
        mine = pl.ds(pl.multiple_of(core * half, half), half)
        acc[mine, :] = acc[mine, :] + recv[...]
        started = []
        for k in range(1, nz):
            at = pl.ds(pl.multiple_of(core * half + zpeer(k) * chunk, chunk), chunk)
            snd[k] = acc[at, :].astype(BF16)
            copy = remote(snd.at[k], rcv.at[k], zs.at[n, k], zr.at[n, k], {"dp": zpeer(k) * 2 + core})
            copy.start()
            started.append(copy)
        return started

    def settle(n, acc, started, rcv, out):
        at = pl.ds(pl.multiple_of(core * half + z * chunk, chunk), chunk)
        total = acc[at, :]
        for k in range(1, nz):
            started[k - 1].wait_recv()
            total = total + rcv[k].astype(F32)
        out[at, :] = (total * scale).astype(BF16)
        sent = []
        for k in range(1, nz):
            copy = remote(
                out.at[at], out.at[at], zs.at[n + 2, k], zr.at[n + 2, k], {"dp": zpeer(k) * 2 + core}
            )
            copy.start()
            sent.append(copy)
        return sent

    def share(n, out):
        for k in range(1, nz):
            at = pl.ds(pl.multiple_of(core * half + zfrom(k) * chunk, chunk), chunk)
            remote(
                out.at[at], out.at[at], zs.at[n + 2, k], zr.at[n + 2, k], {"dp": zpeer(k) * 2 + core}
            ).wait_recv()
        mine = pl.ds(pl.multiple_of(core * half, half), half)
        copy = remote(out.at[mine], out.at[mine], cs.at[n + 2], cr.at[n + 2], {"dp": mate})
        copy.start()
        return copy

    def shared(n, out):
        other = pl.ds(pl.multiple_of((1 - core) * half, half), half)
        remote(out.at[other], out.at[other], cs.at[n + 2], cr.at[n + 2], {"dp": mate}).wait_recv()

    swap2 = swap(1, acc2, half2)
    swap2.start()

    for k in range(1, nf):
        hcopies[k - 1].wait_recv()

    def deltas(q, _):
        at = pl.ds(pl.multiple_of(q * PLANE, PLANE), PLANE)
        grad = hpart[block(f), at]
        for k in range(1, nf):
            grad = grad + hrecv[k, :, at]
        a = first[:, at]
        sg = 1.0 / (1.0 + jnp.exp(-a))
        first[:, at] = grad * sg * (1.0 + a * (1.0 - sg))
        return 0

    lax.fori_loop(0, PLANES, deltas, 0)
    build_stack(c, first, stack)

    swap2.wait_recv()
    spread2 = spread(1, acc2, half2, snd2, rcv2)

    weight_grad(c, stack, xg, acc1)
    swap1 = swap(0, acc1, half1)
    swap1.start()
    backward(w1t, stack, ipart)
    icopies = scatter(3, ipart, irecv)
    for copy in icopies:
        copy.start()

    swap1.wait_recv()
    spread1 = spread(0, acc1, half1, snd1, rcv1)
    sent2 = settle(1, acc2, spread2, rcv2, g2)

    def keep(q, total):
        out[:, pl.ds(pl.multiple_of(q * PLANE, PLANE), PLANE)] = total.astype(BF16)

    forward(c, hg, w2, proj, keep)

    sent1 = settle(0, acc1, spread1, rcv1, g1)
    last2 = share(1, g2)

    for k in range(1, nf):
        icopies[k - 1].wait_recv()

    def inputs(q, _):
        at = pl.ds(pl.multiple_of(q * PLANE, PLANE), PLANE)
        grad = ipart[block(f), at].astype(F32)
        for k in range(1, nf):
            grad = grad + irecv[k, :, at].astype(F32)
        igrad[:, at] = grad.astype(BF16)
        return 0

    lax.fori_loop(0, PLANES, inputs, 0)

    last1 = share(0, g1)
    shared(1, g2)
    shared(0, g1)
    for copy in copies + hcopies + gcopies + icopies + [swap1, swap2] + spread1 + spread2:
        copy.wait_send()
    for copy in sent1 + sent2 + [last1, last2]:
        copy.wait_send()


def one_patch(x, u, w1, w2, nf, nd):
    c = x.shape[0]
    rows = 27 * c
    wide = w1.shape[-1]
    padded = -(-rows // (16 * nd)) * 16 * nd
    half = padded // 2
    nz = nd // 2
    chunk = half // nz
    scale = 1.0 / math.sqrt(nd * CELLS)
    w1 = w1.reshape(rows, wide)
    w2 = w2.reshape(rows, wide)
    vmem = pl.BlockSpec(memory_space=pltpu.VMEM)
    shape = jax.ShapeDtypeStruct
    flops = 12 * rows * wide * CELLS
    return pl.pallas_call(
        functools.partial(kernel, nf, nd, c, scale),
        out_shape=(
            shape((c, CELLS), BF16), shape((c, CELLS), BF16), shape((padded, wide), BF16), shape((padded, wide), BF16)
        ),
        in_specs=[vmem] * 6,
        out_specs=(vmem,) * 4,
        scratch_shapes=[
            pltpu.VMEM((wide, CELLS), BF16),
            pltpu.VMEM((wide, CELLS), BF16),
            pltpu.VMEM((rows, CELLS + 2 * PLANE), BF16),
            pltpu.VMEM((PLANES + 2, rows, PLANE), F32),
            pltpu.VMEM((wide, CELLS), F32),
            pltpu.VMEM((nf, c, CELLS), F32),
            pltpu.VMEM((c, CELLS), F32),
            pltpu.VMEM((wide, CELLS), BF16),
            pltpu.VMEM((nf, c, CELLS), BF16),
            pltpu.VMEM((padded, wide), F32),
            pltpu.VMEM((padded, wide), F32),
            pltpu.VMEM((half, wide), F32),
            pltpu.VMEM((half, wide), F32),
            pltpu.VMEM((nz, chunk, wide), BF16),
            pltpu.VMEM((nz, chunk, wide), BF16),
            pltpu.VMEM((nz, chunk, wide), BF16),
            pltpu.VMEM((nz, chunk, wide), BF16),
            pltpu.SemaphoreType.DMA((4, nf)),
            pltpu.SemaphoreType.DMA((4, nf)),
            pltpu.SemaphoreType.DMA((4,)),
            pltpu.SemaphoreType.DMA((4,)),
            pltpu.SemaphoreType.DMA((4, nz)),
            pltpu.SemaphoreType.DMA((4, nz)),
        ],
        compiler_params=pltpu.CompilerParams(
            collective_id=0, has_side_effects=True, vmem_limit_bytes=60 * 1024 * 1024
        ),
        cost_estimate=pl.CostEstimate(flops=flops, bytes_accessed=16 * 1024 * 1024, transcendentals=0),
    )(x, u, w1, w2, w1.T, w2.T)


def shards(nf, nd, patches, cotangent, first_weight, second_weight, counts):
    c = patches.shape[0]
    every = lax.all_gather(counts, "dp", axis=0, tiled=True)
    me = lax.axis_index("dp")
    offset = jnp.sum(jnp.where(jnp.arange(nd) < me, every, 0))
    slot = jnp.arange(CAP, dtype=jnp.int32)
    live = slot < counts[0]
    target = offset + slot
    pairs = jnp.stack([patches, cotangent])
    hit = (target[None, :] == jnp.arange(nd)[:, None]) & live[None, :]
    placed = jnp.zeros((nd, 2, c, CELLS), BF16)
    for j in range(CAP):
        placed = jnp.where(hit[:, j][:, None, None, None], pairs[None, :, :, j], placed)
    got = lax.psum_scatter(placed, "dp", scatter_dimension=0, tiled=False)
    out, igrad, g1, g2 = one_patch(got[0], got[1], first_weight, second_weight, nf, nd)
    back = lax.all_gather(jnp.stack([out, igrad]), "dp", axis=0, tiled=False)
    outs = []
    for n in range(2):
        columns = []
        for j in range(CAP):
            at = jnp.minimum(target[j], nd - 1)
            block = lax.dynamic_index_in_dim(back[:, n], at, 0, keepdims=False).astype(F32)
            columns.append(jnp.where(live[j], block, 0.0))
        outs.append(jnp.stack(columns, axis=1))
    rows = 27 * c
    shape = first_weight.shape
    return (
        outs[0],
        outs[1],
        g1[:rows].astype(F32).reshape(shape),
        g2[:rows].astype(F32).reshape(shape),
    )


def solution(mesh):
    placed = (
        P("filter", "dp", None),
        P("filter", "dp", None),
        P(None, "filter", None),
        P(None, "filter", None),
        P("dp"),
    )
    return jax.shard_map(
        functools.partial(shards, mesh.shape["filter"], mesh.shape["dp"]),
        mesh=mesh,
        in_specs=placed,
        out_specs=(
            P("filter", "dp", None),
            P("filter", "dp", None),
            P(None, "filter", None),
            P(None, "filter", None),
        ),
        check_vma=False,
    )
```

```python
import functools
import math

import jax
import jax.numpy as jnp
from jax import lax
from jax.experimental import pallas as pl
from jax.experimental.pallas import tpu as pltpu
from jax.sharding import PartitionSpec as P

CAP = 3
CELLS = 2048
PLANE = 256
PLANES = 8
SIDE = 16
MESH = pl.DeviceIdType.MESH
F32 = jnp.float32
BF16 = jnp.bfloat16

PAIRS = [(oy, oz) for oy in (-1, 0, 1) for oz in (-1, 0, 1)]


def inside(oy, oz):
    cell = lax.broadcasted_iota(jnp.int32, (1, PLANE), 1)
    y = cell // SIDE + oy
    z = cell % SIDE + oz
    return (y >= 0) & (y < SIDE) & (z >= 0) & (z < SIDE)


def moved(value, oy, oz):
    step = oy * SIDE + oz
    if step == 0:
        return value
    rolled = pltpu.roll(value, (-step) % PLANE, 1)
    return jnp.where(inside(oy, oz), rolled, jnp.zeros_like(rolled))


def remote(src, dst, send, recv, target):
    return pltpu.make_async_remote_copy(
        src_ref=src, dst_ref=dst, send_sem=send, recv_sem=recv, device_id=target, device_id_type=MESH
    )


def build_stack(c, value, stack):
    zero = jnp.zeros((9 * c, PLANE), BF16)
    stack[:, 0:PLANE] = zero
    stack[:, (PLANES + 1) * PLANE :] = zero

    def plane(p, _):
        part = value[:, pl.ds(pl.multiple_of(p * PLANE, PLANE), PLANE)].astype(F32)
        here = pl.ds(pl.multiple_of((p + 1) * PLANE, PLANE), PLANE)
        for j, (oy, oz) in enumerate(PAIRS):
            stack[j * c : (j + 1) * c, here] = moved(part, -oy, -oz).astype(BF16)
        return 0

    lax.fori_loop(0, PLANES, plane, 0)


def forward(c, value, weight, proj, finish):
    rows = 27 * c
    proj[3, 0 : 9 * c, :] = jnp.zeros((9 * c, PLANE), F32)

    def multiply(p):
        part = value[:, pl.ds(pl.multiple_of(p * PLANE, PLANE), PLANE)]
        proj[lax.rem(p, 4)] = jnp.dot(weight[...], part, preferred_element_type=F32)

    def combine(q):
        total = jnp.zeros((c, PLANE), F32)
        for j, (oy, oz) in enumerate(PAIRS):
            terms = [
                proj[lax.rem(q + 4 + ox, 4), (9 * (ox + 1) + j) * c : (9 * (ox + 1) + j + 1) * c, :]
                for ox in (-1, 0, 1)
            ]
            total = total + moved(terms[0] + terms[1] + terms[2], oy, oz)
        finish(q, total)

    def both(p, _):
        multiply(p)
        combine(p - 2)
        return 0

    multiply(jnp.int32(0))
    multiply(jnp.int32(1))
    lax.fori_loop(2, PLANES, both, 0)
    proj[0, 18 * c : rows, :] = jnp.zeros((9 * c, PLANE), F32)

    def last(q, _):
        combine(q)
        return 0

    lax.fori_loop(PLANES - 2, PLANES, last, 0)


def backward(weight_t, stack, out):
    def plane(q, _):
        part = jnp.concatenate(
            [stack[:, pl.ds(pl.multiple_of((q + 1 - ox) * PLANE, PLANE), PLANE)] for ox in (-1, 0, 1)], axis=0
        )
        value = jnp.dot(weight_t[...], part, preferred_element_type=F32)
        out[:, pl.ds(pl.multiple_of(q * PLANE, PLANE), PLANE)] = value.astype(out.dtype)
        return 0

    lax.fori_loop(0, PLANES, plane, 0)


def weight_grad(c, stack, value, out):
    for part in range(3):
        rows = pl.ds(part * 9 * c, 9 * c)
        out[rows, :] = lax.dot_general(
            stack[:, (2 - part) * PLANE : (2 - part + PLANES) * PLANE],
            value[...],
            (((1,), (1,)), ((), ())),
            preferred_element_type=F32,
        )
    rest = out.shape[0] - 27 * c
    if rest:
        out[27 * c :, :] = jnp.zeros((rest, out.shape[1]), F32)


def cap_right(n, e):
    return jnp.minimum(2 * e, n - e)


def cap_left(n, e):
    return jnp.minimum(2 * (n - e), e)


def most(n):
    return max(min(2 * e, n - e) for e in range(n + 1))


def kernel(
    nf, nd, c, scale,
    cnt, x3, u3, w1, w2, w1t, w2t,
    out, igrad, g1, g2,
    xg, hg, stack, dstack, proj, hpart, hrecv, ipart, irecv, acc1, acc2, half1, half2,
    snd1, snd2, rcv1, rcv2, counts, pre_r, pre_l, got_r, got_l, res, ret_r0, ret_r1, ret_l0, ret_l1,
    fs, fr, cs, cr, zs, zr, ns, nr, rs, rr, ls, lr, brs, brr, bls, blr,
):
    ret_r, ret_l = (ret_r0, ret_r1), (ret_l0, ret_l1)
    x, u, first = irecv.at[0], res.at[0], hrecv.at[0]
    f = lax.axis_index("filter")
    d = lax.axis_index("dp")
    nz = nd // 2
    core = lax.rem(d, 2)
    z = d // 2
    mate = d + 1 - 2 * core
    deep = most(nd)

    def fpeer(k):
        return lax.rem(f + k, nf)

    def ffrom(k):
        return lax.rem(f + nf - k, nf)

    def zpeer(k):
        return lax.rem(z + k, nz)

    def zfrom(k):
        return lax.rem(z + nz - k, nz)

    barrier = pltpu.get_barrier_semaphore()
    for k in range(1, nf):
        pl.semaphore_signal(barrier, inc=1, device_id={"filter": fpeer(k)}, device_id_type=MESH)
    for k in range(1, nd):
        pl.semaphore_signal(barrier, inc=1, device_id={"dp": lax.rem(d + k, nd)}, device_id_type=MESH)
    pl.semaphore_wait(barrier, nf + nd - 2)

    ncopies = [
        remote(cnt, counts.at[d], ns.at[k], nr.at[k], {"dp": lax.rem(d + k, nd)}) for k in range(1, nd)
    ]
    for copy in ncopies:
        copy.start()
    counts[d] = cnt[...]
    for k in range(1, nd):
        remote(
            cnt, counts.at[lax.rem(d + nd - k, nd)], ns.at[k], nr.at[k], {"dp": lax.rem(d + k, nd)}
        ).wait_recv()
    before = jnp.zeros((8, 128), jnp.int32)
    for g in range(nd):
        before = before + counts[g] * (g < d).astype(jnp.int32)
    held = cnt[...][0, 0]
    begin = before[0, 0]
    end = begin + held
    right = jnp.minimum(d + 1, nd - 1)
    left = jnp.maximum(d - 1, 0)

    def stream_r(src, dst, sems, k):
        return remote(src, dst, sems[0].at[k], sems[1].at[k], {"dp": right})

    def stream_l(src, dst, sems, k):
        return remote(src, dst, sems[0].at[k], sems[1].at[k], {"dp": left})

    def balance(n, own3, mine):
        def own(p):
            return own3[jnp.clip(p - begin, 0, CAP - 1)]

        def step(tau, _):
            kr = tau - 2 * d
            kl = tau - 2 * (nd - 1 - d)

            @pl.when((kr >= 0) & (kr < cap_right(nd, d + 1)))
            def _():
                take = kr + 1 < cap_right(nd, d)

                @pl.when(take)
                def _():
                    stream_r(pre_r.at[kr + 1], got_r.at[n, kr + 1], (rs.at[n], rr.at[n]), kr + 1).wait_recv()

                if n:
                    stream_r(pre_r.at[kr], got_r.at[0, kr], (rs.at[0], rr.at[0]), kr).wait_send()
                pre_r[kr] = own(d + 1 + kr)

                @pl.when(take)
                def _():
                    pre_r[kr] = jnp.where(d + 1 + kr < begin, got_r[n, kr + 1], pre_r[kr])

                stream_r(pre_r.at[kr], got_r.at[n, kr], (rs.at[n], rr.at[n]), kr).start()

            @pl.when((kl >= 0) & (kl < cap_left(nd, d)))
            def _():
                take = kl + 1 < cap_left(nd, d + 1)

                @pl.when(take)
                def _():
                    stream_l(pre_l.at[kl + 1], got_l.at[n, kl + 1], (ls.at[n], lr.at[n]), kl + 1).wait_recv()

                if n:
                    stream_l(pre_l.at[kl], got_l.at[0, kl], (ls.at[0], lr.at[0]), kl).wait_send()
                pre_l[kl] = own(d - 1 - kl)

                @pl.when(take)
                def _():
                    pre_l[kl] = jnp.where(d - 1 - kl >= end, got_l[n, kl + 1], pre_l[kl])

                stream_l(pre_l.at[kl], got_l.at[n, kl], (ls.at[n], lr.at[n]), kl).start()

            return 0

        lax.fori_loop(0, 2 * (nd - 1) + deep, step, 0)
        mine[...] = own(d)

        @pl.when(cap_right(nd, d) > 0)
        def _():
            stream_r(pre_r.at[0], got_r.at[n, 0], (rs.at[n], rr.at[n]), 0).wait_recv()
            mine[...] = jnp.where(d < begin, got_r[n, 0], mine[...])

        @pl.when(cap_left(nd, d + 1) > 0)
        def _():
            stream_l(pre_l.at[0], got_l.at[n, 0], (ls.at[n], lr.at[n]), 0).wait_recv()
            mine[...] = jnp.where(d >= end, got_l[n, 0], mine[...])

    def drain_balance(n):
        for k in range(deep):

            @pl.when(k < cap_right(nd, d + 1))
            def _():
                stream_r(pre_r.at[k], got_r.at[n, k], (rs.at[n], rr.at[n]), k).wait_send()

            @pl.when(k < cap_left(nd, d))
            def _():
                stream_l(pre_l.at[k], got_l.at[n, k], (ls.at[n], lr.at[n]), k).wait_send()

    def back_l(n, k):
        src = res.at[n] if k == 0 else ret_l[n].at[k - 1]
        return stream_l(src, ret_l[n].at[k], (bls.at[n], blr.at[n]), k)

    def back_r(n, k):
        src = res.at[n] if k == 0 else ret_r[n].at[k - 1]
        return stream_r(src, ret_r[n].at[k], (brs.at[n], brr.at[n]), k)

    def send_back(n, k):
        @pl.when(k < cap_right(nd, d))
        def _():
            back_l(n, k).start()

        @pl.when(k < cap_left(nd, d + 1))
        def _():
            back_r(n, k).start()

    def receive_back(n, k):
        @pl.when(k < cap_right(nd, d + 1))
        def _():
            back_l(n, k).wait_recv()

        @pl.when(k < cap_left(nd, d))
        def _():
            back_r(n, k).wait_recv()

    def drain_back(n):
        for k in range(deep):

            @pl.when(k < cap_right(nd, d))
            def _():
                back_l(n, k).wait_send()

            @pl.when(k < cap_left(nd, d + 1))
            def _():
                back_r(n, k).wait_send()

    def collect(n, target):
        for j in range(CAP):
            p = begin + j
            value = res[n]
            value = jnp.where(p > d, ret_l[n][jnp.clip(p - d - 1, 0, deep - 1)], value)
            value = jnp.where(p < d, ret_r[n][jnp.clip(d - 1 - p, 0, deep - 1)], value)
            target[j] = jnp.where(j < held, value, jnp.zeros_like(value))

    def block(i):
        return pl.ds(pl.multiple_of(i * c, c), c)

    def gather(n, own, full):
        return [
            remote(own, full.at[block(f)], fs.at[n, k], fr.at[n, k], {"filter": fpeer(k)}) for k in range(1, nf)
        ]

    def gathered(n, own, full):
        for k in range(1, nf):
            remote(own, full.at[block(ffrom(k))], fs.at[n, k], fr.at[n, k], {"filter": fpeer(k)}).wait_recv()

    def scatter(n, part, recv):
        return [
            remote(part.at[block(fpeer(k))], recv.at[k], fs.at[n, k], fr.at[n, k], {"filter": fpeer(k)})
            for k in range(1, nf)
        ]

    half = acc1.shape[0] // 2
    chunk = half // nz

    def swap(n, acc, recv):
        return remote(
            acc.at[pl.ds(pl.multiple_of((1 - core) * half, half), half)],
            recv, cs.at[n], cr.at[n], {"dp": mate},
        )

    def spread(n, acc, recv, snd, rcv):
        mine = pl.ds(pl.multiple_of(core * half, half), half)
        acc[mine, :] = acc[mine, :] + recv[...]
        started = []
        for k in range(1, nz):
            at = pl.ds(pl.multiple_of(core * half + zpeer(k) * chunk, chunk), chunk)
            snd[k] = acc[at, :].astype(BF16)
            copy = remote(snd.at[k], rcv.at[k], zs.at[n, k], zr.at[n, k], {"dp": zpeer(k) * 2 + core})
            copy.start()
            started.append(copy)
        return started

    def settle(n, acc, started, rcv, out):
        at = pl.ds(pl.multiple_of(core * half + z * chunk, chunk), chunk)
        total = acc[at, :]
        for k in range(1, nz):
            started[k - 1].wait_recv()
            total = total + rcv[k].astype(F32)
        out[at, :] = (total * scale).astype(BF16)
        sent = []
        for k in range(1, nz):
            copy = remote(
                out.at[at], out.at[at], zs.at[n + 2, k], zr.at[n + 2, k], {"dp": zpeer(k) * 2 + core}
            )
            copy.start()
            sent.append(copy)
        return sent

    def share(n, out):
        for k in range(1, nz):
            at = pl.ds(pl.multiple_of(core * half + zfrom(k) * chunk, chunk), chunk)
            remote(
                out.at[at], out.at[at], zs.at[n + 2, k], zr.at[n + 2, k], {"dp": zpeer(k) * 2 + core}
            ).wait_recv()
        mine = pl.ds(pl.multiple_of(core * half, half), half)
        copy = remote(out.at[mine], out.at[mine], cs.at[n + 2], cr.at[n + 2], {"dp": mate})
        copy.start()
        return copy

    def shared(n, out):
        other = pl.ds(pl.multiple_of((1 - core) * half, half), half)
        remote(out.at[other], out.at[other], cs.at[n + 2], cr.at[n + 2], {"dp": mate}).wait_recv()

    balance(0, x3, x)
    copies = gather(0, x, xg)
    for copy in copies:
        copy.start()
    xg[block(f), :] = x[...]
    balance(1, u3, u)

    build_stack(c, u, stack)
    backward(w2t, stack, hpart)
    hcopies = scatter(1, hpart, hrecv)
    for copy in hcopies:
        copy.start()

    gathered(0, x, xg)

    def activate(q, total):
        at = pl.ds(pl.multiple_of(q * PLANE, PLANE), PLANE)
        first[:, at] = total
        hg[block(f), at] = (total / (1.0 + jnp.exp(-total))).astype(BF16)

    forward(c, xg, w1, proj, activate)
    own_hidden = hg.at[block(f)]
    gcopies = gather(2, own_hidden, hg)
    for copy in gcopies:
        copy.start()

    for k in range(1, nf):
        hcopies[k - 1].wait_recv()

    def deltas(q, _):
        at = pl.ds(pl.multiple_of(q * PLANE, PLANE), PLANE)
        grad = hpart[block(f), at]
        for k in range(1, nf):
            grad = grad + hrecv[k, :, at]
        a = first[:, at]
        sg = 1.0 / (1.0 + jnp.exp(-a))
        first[:, at] = grad * sg * (1.0 + a * (1.0 - sg))
        return 0

    lax.fori_loop(0, PLANES, deltas, 0)
    build_stack(c, first, dstack)
    backward(w1t, dstack, ipart)
    icopies = scatter(3, ipart, irecv)
    for copy in icopies:
        copy.start()
    weight_grad(c, dstack, xg, acc1)
    swap1 = swap(0, acc1, half1)
    swap1.start()

    gathered(2, own_hidden, hg)
    weight_grad(c, stack, hg, acc2)
    swap2 = swap(1, acc2, half2)
    swap2.start()
    swap1.wait_recv()
    spread1 = spread(0, acc1, half1, snd1, rcv1)

    def keep(q, total):
        res[0, :, pl.ds(pl.multiple_of(q * PLANE, PLANE), PLANE)] = total.astype(BF16)

    forward(c, hg, w2, proj, keep)
    send_back(0, 0)
    swap2.wait_recv()
    spread2 = spread(1, acc2, half2, snd2, rcv2)

    for k in range(1, nf):
        icopies[k - 1].wait_recv()

    def inputs(q, _):
        at = pl.ds(pl.multiple_of(q * PLANE, PLANE), PLANE)
        grad = ipart[block(f), at].astype(F32)
        for k in range(1, nf):
            grad = grad + irecv[k, :, at].astype(F32)
        res[1, :, at] = grad.astype(BF16)
        return 0

    lax.fori_loop(0, PLANES, inputs, 0)
    send_back(1, 0)
    sent1 = settle(0, acc1, spread1, rcv1, g1)
    for n in range(2):
        for k in range(deep):
            receive_back(n, k)
            if k + 1 < deep:
                send_back(n, k + 1)
        if n == 0:
            sent2 = settle(1, acc2, spread2, rcv2, g2)
            last1 = share(0, g1)
            collect(0, out)
    last2 = share(1, g2)
    collect(1, igrad)
    shared(0, g1)
    shared(1, g2)
    for copy in ncopies + copies + hcopies + gcopies + icopies + [swap1, swap2] + spread1 + spread2:
        copy.wait_send()
    for copy in sent1 + sent2 + [last1, last2]:
        copy.wait_send()
    for n in range(2):
        drain_back(n)
    drain_balance(1)


def patches_kernel(cnt, x3, u3, w1, w2, nf, nd):
    c = x3.shape[1]
    deep = most(nd)
    rows = 27 * c
    wide = w1.shape[-1]
    padded = -(-rows // (16 * nd)) * 16 * nd
    half = padded // 2
    nz = nd // 2
    chunk = half // nz
    scale = 1.0 / math.sqrt(nd * CELLS)
    w1 = w1.reshape(rows, wide)
    w2 = w2.reshape(rows, wide)
    vmem = pl.BlockSpec(memory_space=pltpu.VMEM)
    shape = jax.ShapeDtypeStruct
    flops = 12 * rows * wide * CELLS
    return pl.pallas_call(
        functools.partial(kernel, nf, nd, c, scale),
        out_shape=(
            shape((CAP, c, CELLS), BF16), shape((CAP, c, CELLS), BF16), shape((padded, wide), BF16), shape((padded, wide), BF16)
        ),
        in_specs=[vmem] * 7,
        out_specs=(vmem,) * 4,
        scratch_shapes=[
            pltpu.VMEM((wide, CELLS), BF16),
            pltpu.VMEM((wide, CELLS), BF16),
            pltpu.VMEM((9 * c, CELLS + 2 * PLANE), BF16),
            pltpu.VMEM((9 * c, CELLS + 2 * PLANE), BF16),
            pltpu.VMEM((4, rows, PLANE), F32),
            pltpu.VMEM((wide, CELLS), F32),
            pltpu.VMEM((nf, c, CELLS), F32),
            pltpu.VMEM((wide, CELLS), BF16),
            pltpu.VMEM((nf, c, CELLS), BF16),
            pltpu.VMEM((padded, wide), F32),
            pltpu.VMEM((padded, wide), F32),
            pltpu.VMEM((half, wide), F32),
            pltpu.VMEM((half, wide), F32),
            pltpu.VMEM((nz, chunk, wide), BF16),
            pltpu.VMEM((nz, chunk, wide), BF16),
            pltpu.VMEM((nz, chunk, wide), BF16),
            pltpu.VMEM((nz, chunk, wide), BF16),
            pltpu.VMEM((nd, 8, 128), jnp.int32),
            pltpu.VMEM((deep, c, CELLS), BF16),
            pltpu.VMEM((deep, c, CELLS), BF16),
            pltpu.VMEM((2, deep, c, CELLS), BF16),
            pltpu.VMEM((2, deep, c, CELLS), BF16),
            pltpu.VMEM((2, c, CELLS), BF16),
            pltpu.VMEM((deep, c, CELLS), BF16),
            pltpu.VMEM((deep, c, CELLS), BF16),
            pltpu.VMEM((deep, c, CELLS), BF16),
            pltpu.VMEM((deep, c, CELLS), BF16),
            pltpu.SemaphoreType.DMA((4, nf)),
            pltpu.SemaphoreType.DMA((4, nf)),
            pltpu.SemaphoreType.DMA((4,)),
            pltpu.SemaphoreType.DMA((4,)),
            pltpu.SemaphoreType.DMA((4, nz)),
            pltpu.SemaphoreType.DMA((4, nz)),
            pltpu.SemaphoreType.DMA((nd,)),
            pltpu.SemaphoreType.DMA((nd,)),
        ] + [pltpu.SemaphoreType.DMA((2, deep))] * 8,
        compiler_params=pltpu.CompilerParams(
            collective_id=0, has_side_effects=True, vmem_limit_bytes=58 * 1024 * 1024
        ),
        cost_estimate=pl.CostEstimate(flops=flops, bytes_accessed=16 * 1024 * 1024, transcendentals=0),
    )(cnt, x3, u3, w1, w2, w1.T, w2.T)


def shards(nf, nd, patches, cotangent, first_weight, second_weight, counts):
    c = patches.shape[0]
    cnt = jnp.broadcast_to(counts[:, None], (8, 128))
    out, igrad, g1, g2 = patches_kernel(
        cnt, jnp.swapaxes(patches, 0, 1), jnp.swapaxes(cotangent, 0, 1), first_weight, second_weight, nf, nd
    )
    rows = 27 * c
    shape = first_weight.shape
    return (
        jnp.swapaxes(out, 0, 1).astype(F32),
        jnp.swapaxes(igrad, 0, 1).astype(F32),
        g1[:rows].astype(F32).reshape(shape),
        g2[:rows].astype(F32).reshape(shape),
    )


def solution(mesh):
    placed = (
        P("filter", "dp", None),
        P("filter", "dp", None),
        P(None, "filter", None),
        P(None, "filter", None),
        P("dp"),
    )
    return jax.shard_map(
        functools.partial(shards, mesh.shape["filter"], mesh.shape["dp"]),
        mesh=mesh,
        in_specs=placed,
        out_specs=(
            P("filter", "dp", None),
            P("filter", "dp", None),
            P(None, "filter", None),
            P(None, "filter", None),
        ),
        check_vma=False,
    )
```

```python
import functools
import math

import jax
import jax.numpy as jnp
from jax import lax
from jax.experimental import pallas as pl
from jax.experimental.pallas import tpu as pltpu
from jax.sharding import PartitionSpec as P

CAP = 3
CELLS = 2048
PLANE = 256
PLANES = 8
SIDE = 16
MESH = pl.DeviceIdType.MESH
F32 = jnp.float32
BF16 = jnp.bfloat16

PAIRS = [(oy, oz) for oy in (-1, 0, 1) for oz in (-1, 0, 1)]


def inside(oy, oz):
    cell = lax.broadcasted_iota(jnp.int32, (1, PLANE), 1)
    y = cell // SIDE + oy
    z = cell % SIDE + oz
    return (y >= 0) & (y < SIDE) & (z >= 0) & (z < SIDE)


def moved(value, oy, oz):
    step = oy * SIDE + oz
    if step == 0:
        return value
    rolled = pltpu.roll(value, (-step) % PLANE, 1)
    return jnp.where(inside(oy, oz), rolled, jnp.zeros_like(rolled))


def remote(src, dst, send, recv, target):
    return pltpu.make_async_remote_copy(
        src_ref=src, dst_ref=dst, send_sem=send, recv_sem=recv, device_id=target, device_id_type=MESH
    )


def build_stack(c, value, stack):
    zero = jnp.zeros((9 * c, PLANE), BF16)
    stack[:, 0:PLANE] = zero
    stack[:, (PLANES + 1) * PLANE :] = zero

    def plane(p, _):
        part = value[:, pl.ds(pl.multiple_of(p * PLANE, PLANE), PLANE)].astype(F32)
        here = pl.ds(pl.multiple_of((p + 1) * PLANE, PLANE), PLANE)
        for j, (oy, oz) in enumerate(PAIRS):
            stack[j * c : (j + 1) * c, here] = moved(part, -oy, -oz).astype(BF16)
        return 0

    lax.fori_loop(0, PLANES, plane, 0)


def forward(c, value, weight, proj, finish):
    rows = 27 * c
    proj[3, 0 : 9 * c, :] = jnp.zeros((9 * c, PLANE), F32)

    def multiply(p):
        part = value[:, pl.ds(pl.multiple_of(p * PLANE, PLANE), PLANE)]
        proj[lax.rem(p, 4)] = jnp.dot(weight[...], part, preferred_element_type=F32)

    def combine(q):
        total = jnp.zeros((c, PLANE), F32)
        for j, (oy, oz) in enumerate(PAIRS):
            terms = [
                proj[lax.rem(q + 4 + ox, 4), (9 * (ox + 1) + j) * c : (9 * (ox + 1) + j + 1) * c, :]
                for ox in (-1, 0, 1)
            ]
            total = total + moved(terms[0] + terms[1] + terms[2], oy, oz)
        finish(q, total)

    def both(p, _):
        multiply(p)
        combine(p - 2)
        return 0

    multiply(jnp.int32(0))
    multiply(jnp.int32(1))
    lax.fori_loop(2, PLANES, both, 0)
    proj[0, 18 * c : rows, :] = jnp.zeros((9 * c, PLANE), F32)

    def last(q, _):
        combine(q)
        return 0

    lax.fori_loop(PLANES - 2, PLANES, last, 0)


def backward(weight_t, stack, out):
    def plane(q, _):
        part = jnp.concatenate(
            [stack[:, pl.ds(pl.multiple_of((q + 1 - ox) * PLANE, PLANE), PLANE)] for ox in (-1, 0, 1)], axis=0
        )
        value = jnp.dot(weight_t[...], part, preferred_element_type=F32)
        out[:, pl.ds(pl.multiple_of(q * PLANE, PLANE), PLANE)] = value.astype(out.dtype)
        return 0

    lax.fori_loop(0, PLANES, plane, 0)


def weight_grad(c, stack, value, out):
    for part in range(3):
        rows = pl.ds(part * 9 * c, 9 * c)
        out[rows, :] = lax.dot_general(
            stack[:, (2 - part) * PLANE : (2 - part + PLANES) * PLANE],
            value[...],
            (((1,), (1,)), ((), ())),
            preferred_element_type=F32,
        )
    rest = out.shape[0] - 27 * c
    if rest:
        out[27 * c :, :] = jnp.zeros((rest, out.shape[1]), F32)


def most(n):
    return max(min(2 * e, n - e) for e in range(n + 1))


def kernel(
    nf, nd, c, scale, deep,
    every, x3, u3, w1, w2, w1t, w2t,
    out, igrad, g1, g2,
    xg, hg, stack, dstack, proj, hpart, hrecv, ipart, irecv, acc1, acc2, half1, half2,
    snd1, snd2, rcv1, rcv2, pre_r, pre_l, got_r, got_l, res, ret_r0, ret_r1, ret_l0, ret_l1,
    fs, fr, cs, cr, zs, zr, rs, rr, ls, lr, brs, brr, bls, blr,
):
    ret_r, ret_l = (ret_r0, ret_r1), (ret_l0, ret_l1)
    x, u, first = irecv.at[0], res.at[0], hrecv.at[0]
    f = lax.axis_index("filter")
    d = lax.axis_index("dp")
    nz = nd // 2
    core = lax.rem(d, 2)
    z = d // 2
    mate = d + 1 - 2 * core

    def cap_right(n, e):
        return jnp.minimum(jnp.minimum(2 * e, n - e), deep)

    def cap_left(n, e):
        return jnp.minimum(jnp.minimum(2 * (n - e), e), deep)

    def fpeer(k):
        return lax.rem(f + k, nf)

    def ffrom(k):
        return lax.rem(f + nf - k, nf)

    def zpeer(k):
        return lax.rem(z + k, nz)

    def zfrom(k):
        return lax.rem(z + nz - k, nz)

    barrier = pltpu.get_barrier_semaphore()
    for k in range(1, nf):
        pl.semaphore_signal(barrier, inc=1, device_id={"filter": fpeer(k)}, device_id_type=MESH)
    for k in range(1, nd):
        pl.semaphore_signal(barrier, inc=1, device_id={"dp": lax.rem(d + k, nd)}, device_id_type=MESH)
    pl.semaphore_wait(barrier, nf + nd - 2)

    begin = jnp.int32(0)
    for g in range(nd):
        begin = begin + every[g] * (g < d).astype(jnp.int32)
    held = every[d]
    end = begin + held
    right = jnp.minimum(d + 1, nd - 1)
    left = jnp.maximum(d - 1, 0)

    def stream_r(src, dst, sems, k):
        return remote(src, dst, sems[0].at[k], sems[1].at[k], {"dp": right})

    def stream_l(src, dst, sems, k):
        return remote(src, dst, sems[0].at[k], sems[1].at[k], {"dp": left})

    def balance(n, own3, mine):
        def own(p):
            return own3[jnp.clip(p - begin, 0, CAP - 1)]

        def step(tau, _):
            kr = tau - 2 * d
            kl = tau - 2 * (nd - 1 - d)

            @pl.when((kr >= 0) & (kr < cap_right(nd, d + 1)))
            def _():
                take = kr + 1 < cap_right(nd, d)

                @pl.when(take)
                def _():
                    stream_r(pre_r.at[kr + 1], got_r.at[n, kr + 1], (rs.at[n], rr.at[n]), kr + 1).wait_recv()

                if n:
                    stream_r(pre_r.at[kr], got_r.at[0, kr], (rs.at[0], rr.at[0]), kr).wait_send()
                pre_r[kr] = own(d + 1 + kr)

                @pl.when(take)
                def _():
                    pre_r[kr] = jnp.where(d + 1 + kr < begin, got_r[n, kr + 1], pre_r[kr])

                stream_r(pre_r.at[kr], got_r.at[n, kr], (rs.at[n], rr.at[n]), kr).start()

            @pl.when((kl >= 0) & (kl < cap_left(nd, d)))
            def _():
                take = kl + 1 < cap_left(nd, d + 1)

                @pl.when(take)
                def _():
                    stream_l(pre_l.at[kl + 1], got_l.at[n, kl + 1], (ls.at[n], lr.at[n]), kl + 1).wait_recv()

                if n:
                    stream_l(pre_l.at[kl], got_l.at[0, kl], (ls.at[0], lr.at[0]), kl).wait_send()
                pre_l[kl] = own(d - 1 - kl)

                @pl.when(take)
                def _():
                    pre_l[kl] = jnp.where(d - 1 - kl >= end, got_l[n, kl + 1], pre_l[kl])

                stream_l(pre_l.at[kl], got_l.at[n, kl], (ls.at[n], lr.at[n]), kl).start()

            return 0

        lax.fori_loop(0, 2 * (nd - 1) + deep, step, 0)
        mine[...] = own(d)

        @pl.when(cap_right(nd, d) > 0)
        def _():
            stream_r(pre_r.at[0], got_r.at[n, 0], (rs.at[n], rr.at[n]), 0).wait_recv()
            mine[...] = jnp.where(d < begin, got_r[n, 0], mine[...])

        @pl.when(cap_left(nd, d + 1) > 0)
        def _():
            stream_l(pre_l.at[0], got_l.at[n, 0], (ls.at[n], lr.at[n]), 0).wait_recv()
            mine[...] = jnp.where(d >= end, got_l[n, 0], mine[...])

    def drain_balance(n):
        for k in range(deep):

            @pl.when(k < cap_right(nd, d + 1))
            def _():
                stream_r(pre_r.at[k], got_r.at[n, k], (rs.at[n], rr.at[n]), k).wait_send()

            @pl.when(k < cap_left(nd, d))
            def _():
                stream_l(pre_l.at[k], got_l.at[n, k], (ls.at[n], lr.at[n]), k).wait_send()

    def back_l(n, k):
        src = res.at[n] if k == 0 else ret_l[n].at[k - 1]
        return stream_l(src, ret_l[n].at[k], (bls.at[n], blr.at[n]), k)

    def back_r(n, k):
        src = res.at[n] if k == 0 else ret_r[n].at[k - 1]
        return stream_r(src, ret_r[n].at[k], (brs.at[n], brr.at[n]), k)

    def send_back(n, k):
        @pl.when(k < cap_right(nd, d))
        def _():
            back_l(n, k).start()

        @pl.when(k < cap_left(nd, d + 1))
        def _():
            back_r(n, k).start()

    def receive_back(n, k):
        @pl.when(k < cap_right(nd, d + 1))
        def _():
            back_l(n, k).wait_recv()

        @pl.when(k < cap_left(nd, d))
        def _():
            back_r(n, k).wait_recv()

    def drain_back(n):
        for k in range(deep):

            @pl.when(k < cap_right(nd, d))
            def _():
                back_l(n, k).wait_send()

            @pl.when(k < cap_left(nd, d + 1))
            def _():
                back_r(n, k).wait_send()

    def collect(n, target):
        for j in range(CAP):
            p = begin + j
            value = res[n]
            value = jnp.where(p > d, ret_l[n][jnp.clip(p - d - 1, 0, deep - 1)], value)
            value = jnp.where(p < d, ret_r[n][jnp.clip(d - 1 - p, 0, deep - 1)], value)
            target[j] = jnp.where(j < held, value, jnp.zeros_like(value))

    def block(i):
        return pl.ds(pl.multiple_of(i * c, c), c)

    def gather(n, own, full):
        return [
            remote(own, full.at[block(f)], fs.at[n, k], fr.at[n, k], {"filter": fpeer(k)}) for k in range(1, nf)
        ]

    def gathered(n, own, full):
        for k in range(1, nf):
            remote(own, full.at[block(ffrom(k))], fs.at[n, k], fr.at[n, k], {"filter": fpeer(k)}).wait_recv()

    def scatter(n, part, recv):
        return [
            remote(part.at[block(fpeer(k))], recv.at[k], fs.at[n, k], fr.at[n, k], {"filter": fpeer(k)})
            for k in range(1, nf)
        ]

    half = acc1.shape[0] // 2
    chunk = half // nz

    def swap(n, acc, recv):
        return remote(
            acc.at[pl.ds(pl.multiple_of((1 - core) * half, half), half)],
            recv, cs.at[n], cr.at[n], {"dp": mate},
        )

    def spread(n, acc, recv, snd, rcv):
        mine = pl.ds(pl.multiple_of(core * half, half), half)
        acc[mine, :] = acc[mine, :] + recv[...]
        started = []
        for k in range(1, nz):
            at = pl.ds(pl.multiple_of(core * half + zpeer(k) * chunk, chunk), chunk)
            snd[k] = acc[at, :].astype(BF16)
            copy = remote(snd.at[k], rcv.at[k], zs.at[n, k], zr.at[n, k], {"dp": zpeer(k) * 2 + core})
            copy.start()
            started.append(copy)
        return started

    def settle(n, acc, started, rcv, out):
        at = pl.ds(pl.multiple_of(core * half + z * chunk, chunk), chunk)
        total = acc[at, :]
        for k in range(1, nz):
            started[k - 1].wait_recv()
            total = total + rcv[k].astype(F32)
        out[at, :] = (total * scale).astype(BF16)
        sent = []
        for k in range(1, nz):
            copy = remote(
                out.at[at], out.at[at], zs.at[n + 2, k], zr.at[n + 2, k], {"dp": zpeer(k) * 2 + core}
            )
            copy.start()
            sent.append(copy)
        return sent

    def share(n, out):
        for k in range(1, nz):
            at = pl.ds(pl.multiple_of(core * half + zfrom(k) * chunk, chunk), chunk)
            remote(
                out.at[at], out.at[at], zs.at[n + 2, k], zr.at[n + 2, k], {"dp": zpeer(k) * 2 + core}
            ).wait_recv()
        mine = pl.ds(pl.multiple_of(core * half, half), half)
        copy = remote(out.at[mine], out.at[mine], cs.at[n + 2], cr.at[n + 2], {"dp": mate})
        copy.start()
        return copy

    def shared(n, out):
        other = pl.ds(pl.multiple_of((1 - core) * half, half), half)
        remote(out.at[other], out.at[other], cs.at[n + 2], cr.at[n + 2], {"dp": mate}).wait_recv()

    balance(0, x3, x)
    copies = gather(0, x, xg)
    for copy in copies:
        copy.start()
    xg[block(f), :] = x[...]
    balance(1, u3, u)

    build_stack(c, u, stack)
    backward(w2t, stack, hpart)
    hcopies = scatter(1, hpart, hrecv)
    for copy in hcopies:
        copy.start()

    gathered(0, x, xg)

    def activate(q, total):
        at = pl.ds(pl.multiple_of(q * PLANE, PLANE), PLANE)
        first[:, at] = total
        hg[block(f), at] = (total / (1.0 + jnp.exp(-total))).astype(BF16)

    forward(c, xg, w1, proj, activate)
    own_hidden = hg.at[block(f)]
    gcopies = gather(2, own_hidden, hg)
    for copy in gcopies:
        copy.start()

    for k in range(1, nf):
        hcopies[k - 1].wait_recv()

    def deltas(q, _):
        at = pl.ds(pl.multiple_of(q * PLANE, PLANE), PLANE)
        grad = hpart[block(f), at]
        for k in range(1, nf):
            grad = grad + hrecv[k, :, at]
        a = first[:, at]
        sg = 1.0 / (1.0 + jnp.exp(-a))
        first[:, at] = grad * sg * (1.0 + a * (1.0 - sg))
        return 0

    lax.fori_loop(0, PLANES, deltas, 0)
    build_stack(c, first, dstack)
    backward(w1t, dstack, ipart)
    icopies = scatter(3, ipart, irecv)
    for copy in icopies:
        copy.start()
    weight_grad(c, dstack, xg, acc1)
    swap1 = swap(0, acc1, half1)
    swap1.start()

    gathered(2, own_hidden, hg)
    weight_grad(c, stack, hg, acc2)
    swap2 = swap(1, acc2, half2)
    swap2.start()
    swap1.wait_recv()
    spread1 = spread(0, acc1, half1, snd1, rcv1)

    def keep(q, total):
        res[0, :, pl.ds(pl.multiple_of(q * PLANE, PLANE), PLANE)] = total.astype(BF16)

    forward(c, hg, w2, proj, keep)
    send_back(0, 0)
    swap2.wait_recv()
    spread2 = spread(1, acc2, half2, snd2, rcv2)

    for k in range(1, nf):
        icopies[k - 1].wait_recv()

    def inputs(q, _):
        at = pl.ds(pl.multiple_of(q * PLANE, PLANE), PLANE)
        grad = ipart[block(f), at].astype(F32)
        for k in range(1, nf):
            grad = grad + irecv[k, :, at].astype(F32)
        res[1, :, at] = grad.astype(BF16)
        return 0

    lax.fori_loop(0, PLANES, inputs, 0)
    send_back(1, 0)
    sent1 = settle(0, acc1, spread1, rcv1, g1)
    for n in range(2):
        for k in range(deep):
            receive_back(n, k)
            if k + 1 < deep:
                send_back(n, k + 1)
        if n == 0:
            sent2 = settle(1, acc2, spread2, rcv2, g2)
            last1 = share(0, g1)
            collect(0, out)
    last2 = share(1, g2)
    collect(1, igrad)
    shared(0, g1)
    shared(1, g2)
    for copy in copies + hcopies + gcopies + icopies + [swap1, swap2] + spread1 + spread2:
        copy.wait_send()
    for copy in sent1 + sent2 + [last1, last2]:
        copy.wait_send()
    for n in range(2):
        drain_back(n)
    drain_balance(1)


def patches_kernel(every, x3, u3, w1, w2, w1t, w2t, nf, nd, deep):
    c = x3.shape[1]
    rows = 27 * c
    wide = w1.shape[-1]
    padded = -(-rows // (16 * nd)) * 16 * nd
    half = padded // 2
    nz = nd // 2
    chunk = half // nz
    scale = 1.0 / math.sqrt(nd * CELLS)
    vmem = pl.BlockSpec(memory_space=pltpu.VMEM)
    shape = jax.ShapeDtypeStruct
    flops = 12 * rows * wide * CELLS
    return pl.pallas_call(
        functools.partial(kernel, nf, nd, c, scale, deep),
        out_shape=(
            shape((CAP, c, CELLS), BF16), shape((CAP, c, CELLS), BF16), shape((padded, wide), BF16), shape((padded, wide), BF16)
        ),
        in_specs=[pl.BlockSpec(memory_space=pltpu.SMEM)] + [vmem] * 6,
        out_specs=(vmem,) * 4,
        scratch_shapes=[
            pltpu.VMEM((wide, CELLS), BF16),
            pltpu.VMEM((wide, CELLS), BF16),
            pltpu.VMEM((9 * c, CELLS + 2 * PLANE), BF16),
            pltpu.VMEM((9 * c, CELLS + 2 * PLANE), BF16),
            pltpu.VMEM((4, rows, PLANE), F32),
            pltpu.VMEM((wide, CELLS), F32),
            pltpu.VMEM((nf, c, CELLS), F32),
            pltpu.VMEM((wide, CELLS), BF16),
            pltpu.VMEM((nf, c, CELLS), BF16),
            pltpu.VMEM((padded, wide), F32),
            pltpu.VMEM((padded, wide), F32),
            pltpu.VMEM((half, wide), F32),
            pltpu.VMEM((half, wide), F32),
            pltpu.VMEM((nz, chunk, wide), BF16),
            pltpu.VMEM((nz, chunk, wide), BF16),
            pltpu.VMEM((nz, chunk, wide), BF16),
            pltpu.VMEM((nz, chunk, wide), BF16),
            pltpu.VMEM((deep, c, CELLS), BF16),
            pltpu.VMEM((deep, c, CELLS), BF16),
            pltpu.VMEM((2, deep, c, CELLS), BF16),
            pltpu.VMEM((2, deep, c, CELLS), BF16),
            pltpu.VMEM((2, c, CELLS), BF16),
            pltpu.VMEM((deep, c, CELLS), BF16),
            pltpu.VMEM((deep, c, CELLS), BF16),
            pltpu.VMEM((deep, c, CELLS), BF16),
            pltpu.VMEM((deep, c, CELLS), BF16),
            pltpu.SemaphoreType.DMA((4, nf)),
            pltpu.SemaphoreType.DMA((4, nf)),
            pltpu.SemaphoreType.DMA((4,)),
            pltpu.SemaphoreType.DMA((4,)),
            pltpu.SemaphoreType.DMA((4, nz)),
            pltpu.SemaphoreType.DMA((4, nz)),
        ] + [pltpu.SemaphoreType.DMA((2, deep))] * 8,
        compiler_params=pltpu.CompilerParams(
            collective_id=deep, has_side_effects=True, vmem_limit_bytes=58 * 1024 * 1024
        ),
        cost_estimate=pl.CostEstimate(flops=flops, bytes_accessed=16 * 1024 * 1024, transcendentals=0),
    )(every, x3, u3, w1, w2, w1t, w2t)


def shards(nf, nd, patches, cotangent, first_weight, second_weight, counts):
    c = patches.shape[0]
    rows = 27 * c
    every = lax.all_gather(counts, "dp", axis=0, tiled=True)
    spill = jnp.max(jnp.abs(jnp.cumsum(every) - jnp.arange(1, nd + 1, dtype=jnp.int32)))
    w1 = first_weight.reshape(rows, -1)
    w2 = second_weight.reshape(rows, -1)
    args = (every, jnp.swapaxes(patches, 0, 1), jnp.swapaxes(cotangent, 0, 1), w1, w2, w1.T, w2.T)
    levels = [1, 2, most(nd)]
    choice = jnp.where(spill <= 1, 0, jnp.where(spill <= 2, 1, 2)).astype(jnp.int32)
    branches = [functools.partial(patches_kernel, nf=nf, nd=nd, deep=deep) for deep in levels]
    out, igrad, g1, g2 = lax.switch(choice, branches, *args)
    shape = first_weight.shape
    return (
        jnp.swapaxes(out, 0, 1).astype(F32),
        jnp.swapaxes(igrad, 0, 1).astype(F32),
        g1[:rows].astype(F32).reshape(shape),
        g2[:rows].astype(F32).reshape(shape),
    )


def solution(mesh):
    placed = (
        P("filter", "dp", None),
        P("filter", "dp", None),
        P(None, "filter", None),
        P(None, "filter", None),
        P("dp"),
    )
    return jax.shard_map(
        functools.partial(shards, mesh.shape["filter"], mesh.shape["dp"]),
        mesh=mesh,
        in_specs=placed,
        out_specs=(
            P("filter", "dp", None),
            P("filter", "dp", None),
            P(None, "filter", None),
            P(None, "filter", None),
        ),
        check_vma=False,
    )
```
